32 devices in a mesh: head: 2 (over y), ctx: 16 (over z, x, core).
Axes of the slice: x: 2, y: 2, z: 4, core: 2. Of those that a mesh axis runs over, the one named last changes fastest.
Arguments:
- queries: bfloat16 [16384, 4096], P(('ctx', 'head')), may hold values from -8 to 8
- saved_key_rows: bfloat16 [16384, 1024], P(('ctx', 'head')), may hold values from -8 to 8
- saved_value_rows: bfloat16 [16384, 1024], P(('ctx', 'head')), may hold values from -6 to 6
- saved_output: bfloat16 [16384, 4096], P(('ctx', 'head')), may hold values from -1.5 to 1.5
- output_gradient: bfloat16 [16384, 4096], P(('ctx', 'head')), may hold values from -6 to 6
- stripe_order: int32 [16, 1024], P('ctx'), may hold values from 0 to 1023, each once within a row
Outputs:
- query_gradient: bfloat16 [16384, 4096], P(('ctx', 'head'))
- key_grad: bfloat16 [16384, 1024], P(('ctx', 'head'))
- value_grad: bfloat16 [16384, 1024], P(('ctx', 'head'))
The draws below stay inside these ranges and needn't reach their ends.
Inputs may be any that keep to these rules, and one draw needn't show every extreme that they name: Each row of stripe_order holds every number from 0 to 1023 once.
All inputs are finite; a program needn't handle non-finite values.
Results may differ from the reference program's by a relative error of at most 0.0049.
Values may be sent and summed in bfloat16 or wider, within the bound.
No kernel may reach another device: no remote copies, remote signals or barrier semaphores. Data moves between devices by JAX's collectives and lax.ppermute only.
A program may use at most 128 MiB of HBM per device.

```python
import math
import jax
import jax.numpy as jnp
from jax import lax

QUERY_HEADS = 32
KEY_HEADS = 8
HEAD_SIZE = 128
BLOCK_TOKENS = 1024
TAIL_POSITIONS = 256
SEQUENCE_LENGTH = 16384
N_CTX = 16


def draw_queries(key, part):
    base_offset = jnp.clip(jax.random.normal(jax.random.fold_in(key, 21), (SEQUENCE_LENGTH, QUERY_HEADS * HEAD_SIZE), jnp.float32), -6.0, 6.0)
    return base_offset.astype(jnp.bfloat16)


def draw_keys(key, part):
    base_offset = jnp.clip(jax.random.normal(jax.random.fold_in(key, 31), (SEQUENCE_LENGTH, KEY_HEADS * HEAD_SIZE), jnp.float32), -6.0, 6.0)
    return base_offset


def draw_saved_key_rows(key, part):
    return draw_keys(key, part).astype(jnp.bfloat16)


def block_scale(own_key, extent, shards, smallest, high):
    def one(axis_at, parts):
        draws = jax.random.uniform(jax.random.fold_in(jax.random.fold_in(own_key, 6), axis_at), (parts,), jnp.float32, smallest / len(shards), high / len(shards))
        return jnp.repeat(jnp.exp(draws), extent[axis_at] // parts).reshape((-1,) + (1,) * (len(extent) - axis_at - 1))

    loudness = one(*shards[0])
    for cut in shards[1:]:
        loudness = loudness * one(*cut)
    return loudness


def gaussian(key, shape, deviation, reach, shards=(), held_as=jnp.bfloat16):
    values = deviation * jax.random.normal(key, shape, jnp.float32)
    if shards:
        values = values * block_scale(key, shape, shards, -0.22, 0.18)
    return jnp.clip(values, -reach, reach).astype(held_as)


def setup_inputs(seed: int = 0) -> dict:
    key_of = jax.random.split(jax.random.key(seed), 7)
    return {
        "queries": draw_queries(jax.random.fold_in(key_of[6], 71), 0),
        "saved_key_rows": draw_saved_key_rows(jax.random.fold_in(key_of[6], 71), 0),
        "saved_value_rows": gaussian(key_of[2], (SEQUENCE_LENGTH, KEY_HEADS * HEAD_SIZE), 1.0, 6.0, ((0, 32),)),
        "saved_output": gaussian(key_of[3], (SEQUENCE_LENGTH, QUERY_HEADS * HEAD_SIZE), 0.25, 1.5, ((0, 32),)),
        "output_gradient": gaussian(key_of[4], (SEQUENCE_LENGTH, QUERY_HEADS * HEAD_SIZE), 1.0, 6.0, ((0, 32),)),
        "stripe_order": jax.vmap(lambda own: jax.random.permutation(own, BLOCK_TOKENS))(jax.random.split(key_of[5], N_CTX)).reshape((N_CTX, BLOCK_TOKENS)).astype(jnp.int32),
    }


def invert_order(order_row):
    return jnp.zeros((BLOCK_TOKENS,), jnp.int32).at[order_row].set(jnp.arange(BLOCK_TOKENS, dtype=jnp.int32))

def add_rows(target, index, terms):
    return target.at[index].add(terms)

def reference(queries, saved_key_rows, saved_value_rows, saved_output, output_gradient, stripe_order):
    query_groups = QUERY_HEADS // KEY_HEADS
    score_scale = 1.0 / math.sqrt(HEAD_SIZE)
    blocked_queries = queries.reshape(N_CTX, BLOCK_TOKENS, KEY_HEADS, query_groups, HEAD_SIZE)
    gradient_blocks = output_gradient.reshape(N_CTX, BLOCK_TOKENS, KEY_HEADS, query_groups, HEAD_SIZE)
    blocked_keys = saved_key_rows.reshape(N_CTX, BLOCK_TOKENS, KEY_HEADS, HEAD_SIZE)
    blocked_values = saved_value_rows.reshape(N_CTX, BLOCK_TOKENS, KEY_HEADS, HEAD_SIZE)
    inverse = jax.vmap(invert_order)(stripe_order.astype(jnp.int32))
    tail_index = inverse[:, BLOCK_TOKENS - TAIL_POSITIONS:].astype(jnp.int32)
    key_tail = jnp.take_along_axis(blocked_keys, tail_index[:, :, None, None], axis=1)
    value_tail = jnp.take_along_axis(blocked_values, tail_index[:, :, None, None], axis=1)
    key_before = jnp.concatenate([jnp.zeros_like(key_tail[:1]), key_tail[:-1]], axis=0)
    value_before = jnp.concatenate([jnp.zeros_like(value_tail[:1]), value_tail[:-1]], axis=0)
    elementwise_products = saved_output.astype(jnp.float32) * output_gradient.astype(jnp.float32)
    delta_rows = lax.optimization_barrier(jnp.sum(elementwise_products.reshape(SEQUENCE_LENGTH, QUERY_HEADS, HEAD_SIZE), axis=2)).reshape(N_CTX, BLOCK_TOKENS, KEY_HEADS, query_groups)
    block_ids = jnp.arange(N_CTX, dtype=jnp.int32)

    def one_block(items):
        query_b, key_b, key_p, value_b, value_p, grad_b, delta_b, order_b, block_id = items
        query_f = query_b.astype(jnp.float32)
        grad_f = grad_b.astype(jnp.float32)
        keys_all = jnp.concatenate([key_b, key_p], axis=0).astype(jnp.float32)
        values_all = jnp.concatenate([value_b, value_p], axis=0).astype(jnp.float32)
        own_part = order_b[None, :] <= order_b[:, None]
        prev_part = jnp.broadcast_to(block_id > 0, (BLOCK_TOKENS, TAIL_POSITIONS))
        visible = jnp.concatenate([own_part, prev_part], axis=1)
        scores = jnp.einsum('igad,jgd->gaij', query_f, keys_all) * score_scale
        scores = jnp.where(visible, scores, -1e+30)
        row_top = lax.optimization_barrier(jnp.max(scores, axis=-1, keepdims=True))
        expo = jnp.where(visible, jnp.exp(scores - row_top), 0.0)
        probs = expo / lax.optimization_barrier(jnp.sum(expo, axis=-1, keepdims=True))
        probs_b = probs.astype(jnp.bfloat16).astype(jnp.float32)
        dprob = jnp.einsum('igad,jgd->gaij', grad_f, values_all)
        delta_t = jnp.transpose(delta_b, (1, 2, 0))[..., None]
        dscore = (probs * (dprob - delta_t)).astype(jnp.bfloat16).astype(jnp.float32)
        query_g = (jnp.einsum('gaij,jgd->igad', dscore, keys_all) * score_scale).astype(jnp.bfloat16)
        key_g = jnp.einsum('gaij,igad->jgd', dscore, query_f) * score_scale
        value_g = jnp.einsum('gaij,igad->jgd', probs_b, grad_f)
        return (query_g, key_g, value_g)
    query_gradient, key_terms, value_terms = lax.map(one_block, (blocked_queries, blocked_keys, key_before, blocked_values, value_before, gradient_blocks, delta_rows, stripe_order, block_ids))
    zeroed_tail = jnp.zeros((1, TAIL_POSITIONS, KEY_HEADS, HEAD_SIZE), jnp.float32)
    key_back = jnp.concatenate([key_terms[1:, BLOCK_TOKENS:], zeroed_tail], axis=0)
    value_back = jnp.concatenate([value_terms[1:, BLOCK_TOKENS:], zeroed_tail], axis=0)
    key_gradient_total = jax.vmap(add_rows)(key_terms[:, :BLOCK_TOKENS], tail_index, key_back)
    value_gradient_total = jax.vmap(add_rows)(value_terms[:, :BLOCK_TOKENS], tail_index, value_back)
    return (query_gradient.reshape(SEQUENCE_LENGTH, QUERY_HEADS * HEAD_SIZE), key_gradient_total.astype(jnp.bfloat16).reshape(SEQUENCE_LENGTH, KEY_HEADS * HEAD_SIZE), value_gradient_total.astype(jnp.bfloat16).reshape(SEQUENCE_LENGTH, KEY_HEADS * HEAD_SIZE))
```

```python
import functools
import math

import jax
import jax.numpy as jnp
from jax import lax
from jax.experimental import pallas as pl
from jax.experimental.pallas import tpu as pltpu
from jax.sharding import PartitionSpec as P

HEAD_SIZE = 128
GROUP_RATIO = 4
BF16 = jnp.bfloat16
F32 = jnp.float32
VMEM_LIMIT = 60 * 2**20
SCORE_SCALE = 1.0 / math.sqrt(HEAD_SIZE)
EXP2_SCALE = SCORE_SCALE * math.log2(math.e)
HIDDEN = -1e30

NT = (((1,), (1,)), ((), ()))
NN = (((1,), (0,)), ((), ()))


def dot(a, b, dims=NN):
    return lax.dot_general(a, b, dims, preferred_element_type=F32)


def params():
    return pltpu.CompilerParams(vmem_limit_bytes=VMEM_LIMIT)


def key_tile(keys):
    return next(size for size in (640, 256, 128) if keys % size == 0)


def delta_kernel(output_ref, grad_ref, delta_ref):
    for head in range(delta_ref.shape[0]):
        columns = slice(head * HEAD_SIZE, (head + 1) * HEAD_SIZE)
        product = output_ref[:, columns].astype(F32) * grad_ref[:, columns].astype(F32)
        delta_ref[head] = jnp.sum(product.T, axis=0, keepdims=True)


def delta_rows(saved_output, output_gradient):
    rows, width = saved_output.shape
    heads = width // HEAD_SIZE
    step = 8
    block = pl.BlockSpec((rows, step * HEAD_SIZE), lambda i: (0, i))
    return pl.pallas_call(
        delta_kernel,
        grid=(heads // step,),
        in_specs=[block, block],
        out_specs=pl.BlockSpec((step, 1, rows), lambda i: (i, 0, 0)),
        out_shape=jax.ShapeDtypeStruct((heads, 1, rows), F32),
        compiler_params=params(),
        cost_estimate=pl.CostEstimate(
            flops=4 * rows * width, bytes_accessed=4 * rows * width, transcendentals=0
        ),
        name="delta_rows",
    )(saved_output, output_gradient)


def tail_kernel(own_pos, peer_pos, own_kv, peer_kv, tail_kv):
    tail = tail_kv.shape[0]
    first = own_pos.shape[1] + peer_pos.shape[1] - tail

    def picked(pos, kv):
        wanted = first + lax.broadcasted_iota(jnp.int32, (tail, pos.shape[1]), 0)
        return dot((pos[...] == wanted).astype(BF16), kv[...])

    tail_kv[...] = (picked(own_pos, own_kv) + picked(peer_pos, peer_kv)).astype(BF16)


def tail_rows(own_pos, peer_pos, own_kv, peer_kv, tail):
    width = own_kv.shape[1]
    block_rows = own_kv.shape[0] + peer_kv.shape[0]
    return pl.pallas_call(
        tail_kernel,
        out_shape=jax.ShapeDtypeStruct((tail, width), BF16),
        compiler_params=params(),
        cost_estimate=pl.CostEstimate(
            flops=2 * tail * block_rows * width,
            bytes_accessed=2 * (tail + block_rows) * width,
            transcendentals=0,
        ),
        name="tail_rows",
    )(own_pos, peer_pos, own_kv, peer_kv)


def group_kernel(
    key_pos, query_pos, queries, grads, delta, own_k, own_v, peer_k, peer_v, tail_k, tail_v, *rest
):
    (dq, own_dk, own_dv, peer_dk, peer_dv, tail_dk, tail_dv) = rest[-19:-12]
    (k_all, kt_all, v_all, bias, dk, dv) = rest[-12:-6]
    scores, probs, dscores = rest[-6:-4], rest[-4:-2], rest[-2:]
    rows = queries.shape[0]
    keys = k_all.shape[0]
    own, peer = own_k.shape[0], peer_k.shape[0]
    query_tile = min(256, rows)
    query_tiles = rows // query_tile
    steps = queries.shape[1] // HEAD_SIZE * query_tiles
    tile = key_tile(keys)
    blocks = [slice(at, at + tile) for at in range(0, keys, tile)]

    @pl.when(pl.program_id(0) == 0)
    def _():
        bias[...] = jnp.where(key_pos[...] <= query_pos[...], 0.0, HIDDEN).astype(F32)

    for whole, parts in ((k_all, (own_k, peer_k, tail_k)), (v_all, (own_v, peer_v, tail_v))):
        at = 0
        for part in parts:
            whole[at : at + part.shape[0]] = part[...]
            at += part.shape[0]
    kt_all[...] = k_all[...].astype(F32).T.astype(BF16)
    top, inverse_sum = {}, {}

    def place(step):
        head, at = divmod(step, query_tiles)
        return (
            slice(at * query_tile, (at + 1) * query_tile),
            slice(head * HEAD_SIZE, (head + 1) * HEAD_SIZE),
        )

    def fold(x):
        return x.reshape(tile // 8, 8, query_tile)

    def score_block(step, block):
        at, columns = place(step)
        s = dot(k_all[block], queries[at, columns], NT) * EXP2_SCALE + bias[block, at]
        scores[step % 2][block] = s
        high = jnp.max(fold(s), axis=0)
        top[step] = jnp.maximum(top[step], high) if step in top else high

    def exp_block(step, block):
        e = jnp.exp2(scores[step % 2][block] - top[step])
        scores[step % 2][block] = e
        total = jnp.sum(fold(e), axis=0)
        inverse_sum[step] = inverse_sum[step] + total if step in inverse_sum else total

    def dscore_block(step, block):
        at, columns = place(step)
        p = scores[step % 2][block] * inverse_sum[step]
        dprob = dot(v_all[block], grads[at, columns], NT)
        probs[step % 2][block] = p.astype(BF16)
        dscores[step % 2][block] = (p * (dprob - delta[step // query_tiles, :, at])).astype(BF16)

    def key_block(step, block):
        at, columns = place(step)
        value_term = dot(probs[step % 2][block], grads[at, columns])
        key_term = dot(dscores[step % 2][block], queries[at, columns])
        if step == 0:
            dv[block] = value_term
            dk[block] = key_term
        else:
            dv[block] += value_term
            dk[block] += key_term

    for block in blocks:
        score_block(0, block)
    for step in range(steps + 1):
        if step < steps:
            top[step] = jnp.max(top[step], axis=0, keepdims=True)
        for block in blocks:
            if step < steps:
                exp_block(step, block)
            if step > 0:
                key_block(step - 1, block)
        if step > 0:
            at, columns = place(step - 1)
            dq_t = dot(kt_all[...], dscores[(step - 1) % 2][...])
            dq[at, columns] = (dq_t * SCORE_SCALE).T.astype(BF16)
        if step < steps:
            inverse_sum[step] = 1.0 / jnp.sum(inverse_sum[step], axis=0, keepdims=True)
        for block in blocks:
            if step + 1 < steps:
                score_block(step + 1, block)
            if step < steps:
                dscore_block(step, block)

    own_dk[...] = dk[:own] * SCORE_SCALE
    own_dv[...] = dv[:own]
    peer_dk[...] = dk[own : own + peer] * SCORE_SCALE
    peer_dv[...] = dv[own : own + peer]
    tail_dk[...] = (dk[own + peer :] * SCORE_SCALE).astype(BF16)
    tail_dv[...] = dv[own + peer :].astype(BF16)


def group_gradients(
    key_pos, query_pos, queries, grads, delta, keys, values, peer_kv, tail_kv, dq, first, count
):
    rows, width = queries.shape
    peer, tail = peer_kv.shape[0], tail_kv.shape[0]
    total = rows + peer + tail
    group = GROUP_RATIO * HEAD_SIZE
    query_tile = min(256, rows)
    query_spec = pl.BlockSpec((rows, group), lambda g: (0, first + g))
    full = pl.BlockSpec((rows, HEAD_SIZE), lambda g: (0, first + g))

    def halves(n):
        return [
            pl.BlockSpec((n, HEAD_SIZE), lambda g: (0, g)),
            pl.BlockSpec((n, HEAD_SIZE), lambda g: (0, count + g)),
        ]

    def one(n):
        return pl.BlockSpec((n, HEAD_SIZE), lambda g: (0, g))

    def shape(n, dtype):
        return jax.ShapeDtypeStruct((n, count * HEAD_SIZE), dtype)

    in_specs = [
        pl.BlockSpec((total, 1), lambda g: (0, 0)),
        pl.BlockSpec((1, rows), lambda g: (0, 0)),
        query_spec,
        query_spec,
        pl.BlockSpec((GROUP_RATIO, 1, rows), lambda g: (first + g, 0, 0)),
        full,
        full,
        *halves(peer),
        *halves(tail),
    ]
    operands = [
        key_pos, query_pos, queries, grads, delta, keys, values, peer_kv, peer_kv, tail_kv, tail_kv
    ]
    aliases = {}
    if dq is not None:
        aliases = {len(operands): 0}
        operands.append(dq)
        in_specs.append(pl.BlockSpec(memory_space=pl.ANY))
    pairs = total * rows * GROUP_RATIO * count
    return pl.pallas_call(
        group_kernel,
        grid=(count,),
        in_specs=in_specs,
        out_specs=[query_spec] + [one(n) for n in (rows, rows, peer, peer, tail, tail)],
        out_shape=[jax.ShapeDtypeStruct((rows, width), BF16)]
        + [shape(n, F32) for n in (rows, rows, peer, peer)]
        + [shape(tail, BF16)] * 2,
        scratch_shapes=[
            pltpu.VMEM((total, HEAD_SIZE), BF16),
            pltpu.VMEM((HEAD_SIZE, total), BF16),
            pltpu.VMEM((total, HEAD_SIZE), BF16),
            pltpu.VMEM((total, rows), F32),
            pltpu.VMEM((total, HEAD_SIZE), F32),
            pltpu.VMEM((total, HEAD_SIZE), F32),
            *[pltpu.VMEM((total, query_tile), F32)] * 2,
            *[pltpu.VMEM((total, query_tile), BF16)] * 4,
        ],
        input_output_aliases=aliases,
        compiler_params=params(),
        cost_estimate=pl.CostEstimate(
            flops=20 * pairs * HEAD_SIZE,
            bytes_accessed=6 * rows * group * count,
            transcendentals=pairs,
        ),
        name="group_gradients",
    )(*operands)


def spread(pos, first, terms):
    wanted = first + lax.broadcasted_iota(jnp.int32, (pos.shape[0], terms.shape[0]), 1)
    return dot((pos[...] == wanted).astype(BF16), terms[...])


def share_kernel(first, pos, peer_dk, peer_dv, back_dk, back_dv, shared):
    width = peer_dk.shape[1]
    shared[:, :width] = (peer_dk[...] + spread(pos, first, back_dk)).astype(BF16)
    shared[:, width:] = (peer_dv[...] + spread(pos, first, back_dv)).astype(BF16)


def peers_share(peer_pos, peer_dk, peer_dv, back_dk, back_dv, first):
    peer, width = peer_dk.shape
    tail = back_dk.shape[0]
    return pl.pallas_call(
        functools.partial(share_kernel, first),
        out_shape=jax.ShapeDtypeStruct((peer, 2 * width), BF16),
        compiler_params=params(),
        cost_estimate=pl.CostEstimate(
            flops=4 * tail * peer * width, bytes_accessed=12 * peer * width, transcendentals=0
        ),
        name="peers_share",
    )(peer_pos, peer_dk, peer_dv, back_dk, back_dv)


def total_kernel(first, pos, own_dk, own_dv, back_dk, back_dv, *rest):
    shares, (key_grad, value_grad) = rest[:-4], rest[-2:]
    width = own_dk.shape[1]
    key_total = own_dk[...] + spread(pos, first, back_dk)
    value_total = own_dv[...] + spread(pos, first, back_dv)
    for share in shares:
        key_total += share[:, :width].astype(F32)
        value_total += share[:, width:].astype(F32)
    key_grad[...] = key_total.astype(BF16)
    value_grad[...] = value_total.astype(BF16)


def total_gradients(own_pos, own_dk, own_dv, back_dk, back_dv, shares, outs, first, at, width):
    rows, part = own_dk.shape
    tail = back_dk.shape[0]
    operands = [own_pos, own_dk, own_dv, back_dk, back_dv, *shares]
    whole = lambda x: pl.BlockSpec(x.shape, lambda i: (0, 0))
    in_specs = [whole(x) for x in operands]
    kernel = functools.partial(total_kernel, first)
    aliases = {len(operands): 0, len(operands) + 1: 1}
    operands += outs
    in_specs += [pl.BlockSpec(memory_space=pl.ANY)] * 2
    out = pl.BlockSpec((rows, part), lambda i: (0, at // part))
    return pl.pallas_call(
        kernel,
        grid=(1,),
        in_specs=in_specs,
        out_specs=[out, out],
        out_shape=[jax.ShapeDtypeStruct((rows, width), BF16)] * 2,
        input_output_aliases=aliases,
        compiler_params=params(),
        cost_estimate=pl.CostEstimate(
            flops=4 * tail * rows * part, bytes_accessed=12 * rows * part, transcendentals=0
        ),
        name="total_gradients",
    )(*operands)


def shifted(x, axis, by):
    peers = lax.axis_size(axis)
    pairs = [(i, i + by) for i in range(peers) if 0 <= i + by < peers]
    return lax.ppermute(x, axis, pairs)


def turned(x, axis, by):
    peers = lax.axis_size(axis)
    return lax.ppermute(x, axis, [(i, (i + by) % peers) for i in range(peers)])


CHUNKS = (2, 2, 2, 2)


def body(queries, saved_key_rows, saved_value_rows, saved_output, output_gradient, stripe_order):
    peers = lax.axis_size("head")
    rows = queries.shape[0]
    width = saved_key_rows.shape[1]
    block_rows = rows * peers
    tail = block_rows // 4
    first_tail = block_rows - tail
    me = lax.axis_index("head")
    order = stripe_order[0]
    order = order.reshape(peers, rows)
    order = jnp.concatenate(
        [lax.dynamic_slice_in_dim(order, (me - by) % peers, 1, 0) for by in range(peers)]
    ).reshape(block_rows)
    own_order, peer_order = order[:rows], order[rows:]
    tail_pos = jnp.where(lax.axis_index("ctx") > 0, -1, block_rows)
    key_pos = jnp.concatenate([order, jnp.full((tail,), tail_pos, jnp.int32)])[:, None]
    query_pos = own_order[None]

    spans, at = [], 0
    for count in CHUNKS:
        spans.append((at, count))
        at += count
    cut = lambda x, first, count: x[:, first * HEAD_SIZE : (first + count) * HEAD_SIZE]
    own_kv = [
        jnp.concatenate([cut(saved_key_rows, *span), cut(saved_value_rows, *span)], axis=1)
        for span in spans
    ]
    peer_kv = [
        jnp.concatenate([turned(x, "head", by) for by in range(1, peers)]) for x in own_kv
    ]
    delta = delta_rows(saved_output, output_gradient)
    tail_kv = [
        shifted(tail_rows(own_order[None], peer_order[None], own, peer, tail), "ctx", 1)
        for own, peer in zip(own_kv, peer_kv)
    ]
    dq = None
    outs = [jnp.zeros((rows, width), BF16)] * 2
    for (first, count), peer, late in zip(spans, peer_kv, tail_kv):
        dq, own_dk, own_dv, peer_dk, peer_dv, tail_dk, tail_dv = group_gradients(
            key_pos, query_pos, queries, output_gradient, delta, saved_key_rows,
            saved_value_rows, peer, late, dq, first, count,
        )
        back_dk, back_dv = shifted((tail_dk, tail_dv), "ctx", -1)
        shared = peers_share(peer_order[:, None], peer_dk, peer_dv, back_dk, back_dv, first_tail)
        shares = [
            turned(shared[(by - 1) * rows : by * rows], "head", -by) for by in range(1, peers)
        ]
        outs = total_gradients(
            own_order[:, None], own_dk, own_dv, back_dk, back_dv, shares, outs,
            first_tail, first * HEAD_SIZE, width,
        )
    return (dq, *outs)


def solution(mesh):
    tokens = P(("ctx", "head"), None)
    return jax.shard_map(
        body,
        mesh=mesh,
        in_specs=(tokens, tokens, tokens, tokens, tokens, P("ctx", None)),
        out_specs=(tokens, tokens, tokens),
        check_vma=False,
    )
```

```python
import functools
import math

import jax
import jax.numpy as jnp
from jax import lax
from jax.experimental import pallas as pl
from jax.experimental.pallas import tpu as pltpu
from jax.sharding import PartitionSpec as P

HEAD_SIZE = 128
GROUP_RATIO = 4
BF16 = jnp.bfloat16
F32 = jnp.float32
VMEM_LIMIT = 23 * 2**20
SCORE_SCALE = 1.0 / math.sqrt(HEAD_SIZE)
EXP2_SCALE = SCORE_SCALE * math.log2(math.e)
HIDDEN = -1e30
PAIR = 2 * HEAD_SIZE
SHORT = pl.CostEstimate(flops=1, bytes_accessed=1, transcendentals=0)

NT = (((1,), (1,)), ((), ()))
NN = (((1,), (0,)), ((), ()))


def dot(a, b, dims=NN):
    return lax.dot_general(a, b, dims, preferred_element_type=F32)


def params():
    return pltpu.CompilerParams(vmem_limit_bytes=VMEM_LIMIT)


def key_tile(keys):
    return next(size for size in (640, 256, 128) if keys % size == 0)


def positions(order, rows):
    me, peers = lax.axis_index("head"), lax.axis_size("head")
    at = [lax.rem(me + peers - by, peers) * rows for by in range(peers)]
    parts = [order[:, pl.ds(pl.multiple_of(x, 128), rows)] for x in at]
    return parts[0], jnp.concatenate(parts[1:], axis=1)


def one_hot(pos, first, tail):
    wanted = first + lax.broadcasted_iota(jnp.int32, (tail, pos.shape[1]), 0)
    return (pos == wanted).astype(BF16)


def pair_kernel(first_tail, start, sizes, tails, keys, values, *refs):
    outs = refs[-len(sizes + tails) :]
    heads = [(out, at) for out, size in zip(outs, sizes) for at in range(size)]
    for head, (out, at) in enumerate(heads, start):
        columns = slice(head * HEAD_SIZE, (head + 1) * HEAD_SIZE)
        out[:, at * PAIR : at * PAIR + HEAD_SIZE] = keys[:, columns]
        out[:, at * PAIR + HEAD_SIZE : (at + 1) * PAIR] = values[:, columns]
    if tails:
        own_pos, _ = positions(refs[0], keys.shape[0])
        picks = one_hot(own_pos, first_tail, outs[-1].shape[0])
        heads = [(out, at) for out, size in zip(outs[len(sizes) :], tails) for at in range(size)]
        for head, (out, at) in enumerate(heads):
            columns = slice(head * HEAD_SIZE, (head + 1) * HEAD_SIZE)
            for side, x in enumerate((keys, values)):
                lane = at * PAIR + side * HEAD_SIZE
                out[:, lane : lane + HEAD_SIZE] = dot(picks, x[:, columns]).astype(BF16)


def paired(keys, values, first_tail, tail, start, sizes, tails, pos, others):
    rows, width = keys.shape
    shapes = [(rows, n * PAIR) for n in sizes] + [(tail, n * PAIR) for n in tails]
    used = max(start + sum(sizes), sum(tails)) * HEAD_SIZE
    block = pl.BlockSpec((rows, used), lambda i: (0, 0))
    whole = lambda x: pl.BlockSpec(x.shape, lambda i: (0, 0))
    shapes = [jax.ShapeDtypeStruct(shape, BF16) for shape in shapes]
    return pl.pallas_call(
        functools.partial(pair_kernel, first_tail, start, sizes, tails),
        grid=(1,),
        in_specs=[block, block, *map(whole, pos)]
        + [pl.BlockSpec(memory_space=pl.ANY)] * len(others),
        out_specs=[whole(x) for x in shapes],
        out_shape=shapes,
        compiler_params=params(),
        cost_estimate=SHORT,
        name="paired",
    )(keys, values, *pos, *others)


def group_kernel(
    first_tail, order, order_before, queries, grads, outputs, own_k, own_v, peer_kv, own_tail,
    before_kv, *rest
):
    (k_all, kt_all, v_all, bias, dk, dv) = rest[-12:-6]
    delta = {}
    scores, probs, dscores = rest[-6:-4], rest[-4:-2], rest[-2:]
    (dq, own_terms, peer_terms, tail_terms) = rest[-16:-12]
    rows = queries.shape[0]
    keys = k_all.shape[0]
    own, peer = own_k.shape[0], peer_kv.shape[0]
    query_tile = min(256, rows)
    query_tiles = rows // query_tile
    steps = queries.shape[1] // HEAD_SIZE * query_tiles
    tile = key_tile(keys)
    blocks = [slice(at, at + tile) for at in range(0, keys, tile)]

    @pl.when(pl.program_id(0) == 0)
    def _():
        query_pos, peer_pos = positions(order, rows)
        late_pos = jnp.where(lax.axis_index("ctx") > 0, -1, own + peer)
        late_pos = jnp.full((1, own_tail.shape[0]), late_pos, jnp.int32)
        key_pos = jnp.concatenate([query_pos, peer_pos, late_pos], axis=1).astype(F32)
        column = jnp.broadcast_to(key_pos, (8, keys)).T[:, :1]
        bias[...] = jnp.where(column <= query_pos.astype(F32), 0.0, HIDDEN)

    for whole, mine, side in ((k_all, own_k, 0), (v_all, own_v, HEAD_SIZE)):
        whole[:own] = mine[...]
        whole[own : own + peer] = peer_kv[:, side : side + HEAD_SIZE]
    tail = own_tail.shape[0]
    _, before_pos = positions(order_before, rows)
    late = own_tail[...].astype(F32) + dot(one_hot(before_pos, first_tail, tail), before_kv[...])
    k_all[own + peer :] = late[:, :HEAD_SIZE].astype(BF16)
    v_all[own + peer :] = late[:, HEAD_SIZE:].astype(BF16)
    kt_all[...] = k_all[...].astype(F32).T.astype(BF16)
    top, inverse_sum = {}, {}

    def place(step):
        head, at = divmod(step, query_tiles)
        return (
            slice(at * query_tile, (at + 1) * query_tile),
            slice(head * HEAD_SIZE, (head + 1) * HEAD_SIZE),
        )

    def fold(x):
        return x.reshape(tile // 8, 8, query_tile)

    def score_block(step, block):
        at, columns = place(step)
        s = dot(k_all[block], queries[at, columns], NT) * EXP2_SCALE + bias[block, at]
        scores[step % 2][block] = s
        high = jnp.max(fold(s), axis=0)
        top[step] = jnp.maximum(top[step], high) if step in top else high

    def delta_row(step):
        at, columns = place(step)
        product = outputs[at, columns].astype(F32) * grads[at, columns].astype(F32)
        delta[step] = jnp.sum(product.T, axis=0, keepdims=True)

    def exp_block(step, block):
        e = jnp.exp2(scores[step % 2][block] - top[step])
        scores[step % 2][block] = e
        total = jnp.sum(fold(e), axis=0)
        inverse_sum[step] = inverse_sum[step] + total if step in inverse_sum else total

    def dscore_block(step, block):
        at, columns = place(step)
        p = scores[step % 2][block] * inverse_sum[step]
        dprob = dot(v_all[block], grads[at, columns], NT)
        probs[step % 2][block] = p.astype(BF16)
        dscores[step % 2][block] = (p * (dprob - delta[step])).astype(BF16)

    def key_block(step, block):
        at, columns = place(step)
        value_term = dot(probs[step % 2][block], grads[at, columns])
        key_term = dot(dscores[step % 2][block], queries[at, columns])
        if step == 0:
            dv[block] = value_term
            dk[block] = key_term
        else:
            dv[block] += value_term
            dk[block] += key_term

    for block in blocks:
        score_block(0, block)
    for step in range(steps + 1):
        if step < steps:
            top[step] = jnp.max(top[step], axis=0, keepdims=True)
            delta_row(step)
        for block in blocks:
            if step < steps:
                exp_block(step, block)
            if step > 0:
                key_block(step - 1, block)
        if step > 0:
            at, columns = place(step - 1)
            dq_t = dot(kt_all[...], dscores[(step - 1) % 2][...])
            dq[at, columns] = (dq_t * SCORE_SCALE).T.astype(BF16)
        if step < steps:
            inverse_sum[step] = 1.0 / jnp.sum(inverse_sum[step], axis=0, keepdims=True)
        for block in blocks:
            if step + 1 < steps:
                score_block(step + 1, block)
            if step < steps:
                dscore_block(step, block)

    for whole, side, scale in ((dk, 0, SCORE_SCALE), (dv, HEAD_SIZE, 1.0)):
        columns = slice(side, side + HEAD_SIZE)
        own_terms[:, columns] = whole[:own] * scale
        peer_terms[:, columns] = whole[own : own + peer] * scale
        tail_terms[:, columns] = (whole[own + peer :] * scale).astype(BF16)


def group_gradients(
    first_tail, order, order_before, queries, grads, outputs, keys, values, peer_kv,
    own_tail, before_kv, first, count, dq, terms, terms_first, terms_count, others,
):
    rows, width = queries.shape
    (peer_kv, peer_first), (own_tail, tail_first), (before_kv, before_first) = (
        peer_kv, own_tail, before_kv
    )
    peer, tail = peer_kv.shape[0], own_tail.shape[0]
    total = rows + peer + tail
    group = GROUP_RATIO * HEAD_SIZE
    query_tile = min(256, rows)
    query_spec = pl.BlockSpec((rows, group), lambda g: (0, first + g))
    own_spec = pl.BlockSpec((rows, HEAD_SIZE), lambda g: (0, first + g))

    def pair_spec(n, start):
        return pl.BlockSpec((n, PAIR), lambda g: (0, first - start + g))

    whole = lambda x: pl.BlockSpec(x.shape, lambda g: (0, 0))
    in_specs = [
        whole(order),
        whole(order_before),
        query_spec,
        query_spec,
        query_spec,
        own_spec,
        own_spec,
        pair_spec(peer, peer_first),
        pair_spec(tail, tail_first),
        pair_spec(peer, before_first),
    ]
    operands = [
        order, order_before, queries, grads, outputs, keys, values, peer_kv, own_tail, before_kv,
    ]
    out_specs = [query_spec] + [pair_spec(n, terms_first) for n in (rows, peer, tail)]
    out_shape = [
        jax.ShapeDtypeStruct((rows, width), BF16),
        jax.ShapeDtypeStruct((rows, terms_count * PAIR), F32),
        jax.ShapeDtypeStruct((peer, terms_count * PAIR), F32),
        jax.ShapeDtypeStruct((tail, terms_count * PAIR), BF16),
    ]
    aliases = {}
    for at, buffer in enumerate((dq, *terms)):
        if buffer is not None:
            aliases[len(operands)] = at
            operands.append(buffer)
    operands += others
    in_specs += [pl.BlockSpec(memory_space=pl.ANY)] * (len(operands) - len(in_specs))
    pairs = total * rows * GROUP_RATIO * count
    return pl.pallas_call(
        functools.partial(group_kernel, first_tail),
        grid=(count,),
        in_specs=in_specs,
        out_specs=out_specs,
        out_shape=out_shape,
        scratch_shapes=[
            pltpu.VMEM((total, HEAD_SIZE), BF16),
            pltpu.VMEM((HEAD_SIZE, total), BF16),
            pltpu.VMEM((total, HEAD_SIZE), BF16),
            pltpu.VMEM((total, rows), F32),
            pltpu.VMEM((total, HEAD_SIZE), F32),
            pltpu.VMEM((total, HEAD_SIZE), F32),
            *[pltpu.VMEM((total, query_tile), F32)] * 2,
            *[pltpu.VMEM((total, query_tile), BF16)] * 4,
        ],
        input_output_aliases=aliases,
        compiler_params=params(),
        cost_estimate=pl.CostEstimate(
            flops=20 * pairs * HEAD_SIZE,
            bytes_accessed=6 * rows * group * count,
            transcendentals=pairs,
        ),
        name="group_gradients",
    )(*operands)


def spread(first, pos, terms):
    picks = one_hot(pos, first, terms.shape[0]).astype(F32).T.astype(BF16)
    return dot(picks, terms[...])


def share_kernel(first, rows, order, peer_terms, back, shared):
    _, pos = positions(order, rows)
    shared[...] = (peer_terms[...] + spread(first, pos, back)).astype(BF16)


def peers_share(first, rows, order, peer_terms, back):
    return pl.pallas_call(
        functools.partial(share_kernel, first, rows),
        out_shape=jax.ShapeDtypeStruct(peer_terms.shape, BF16),
        compiler_params=params(),
        cost_estimate=SHORT,
        name="peers_share",
    )(order, peer_terms, back)


def total_kernel(first, peers, order, own_terms, back, *rest):
    shares, (key_grad, value_grad) = rest[: peers - 1], rest[-2:]
    pos, _ = positions(order, own_terms.shape[0])
    total = own_terms[...] + spread(first, pos, back)
    for share in shares:
        total += share[...].astype(F32)
    for at in range(total.shape[1] // PAIR):
        columns = slice(at * HEAD_SIZE, (at + 1) * HEAD_SIZE)
        key_grad[:, columns] = total[:, at * PAIR : at * PAIR + HEAD_SIZE].astype(BF16)
        value_grad[:, columns] = total[:, at * PAIR + HEAD_SIZE : (at + 1) * PAIR].astype(BF16)


def total_gradients(order, own_terms, back, shares, outs, first_tail, first, width):
    rows, part = own_terms.shape
    count = part // PAIR
    step = count if first % count == 0 else 1
    one = lambda x: pl.BlockSpec((x.shape[0], step * PAIR), lambda g: (0, g))
    operands = [order, own_terms, back, *shares]
    in_specs = [pl.BlockSpec(order.shape, lambda g: (0, 0)), *map(one, operands[1:])]
    aliases = {}
    if outs is not None:
        aliases = {len(operands): 0, len(operands) + 1: 1}
        operands += outs
        in_specs += [pl.BlockSpec(memory_space=pl.ANY)] * 2
    out = pl.BlockSpec((rows, step * HEAD_SIZE), lambda g: (0, first // step + g))
    return pl.pallas_call(
        functools.partial(total_kernel, first_tail, len(shares) + 1),
        grid=(count // step,),
        in_specs=in_specs,
        out_specs=[out, out],
        out_shape=[jax.ShapeDtypeStruct((rows, width), BF16)] * 2,
        input_output_aliases=aliases,
        compiler_params=params(),
        cost_estimate=SHORT,
        name="total_gradients",
    )(*operands)


def shifted(x, axis, by):
    peers = lax.axis_size(axis)
    pairs = [(i, i + by) for i in range(peers) if 0 <= i + by < peers]
    return lax.ppermute(x, axis, pairs)


def turned(x, axis, by):
    peers = lax.axis_size(axis)
    return lax.ppermute(x, axis, [(i, (i + by) % peers) for i in range(peers)])


def spans(sizes):
    return [(sum(sizes[:i]), size) for i, size in enumerate(sizes)]


def after(x, *others):
    return lax.optimization_barrier((x, *others))[0]


FORWARD = (1, 1, 2, 4)
KERNELS = (1, 1, 1, 1, 2, 1, 1)
BACK = (4, 2, 2)
STARTS = (1, 3)


def body(queries, saved_key_rows, saved_value_rows, saved_output, output_gradient, stripe_order):
    peers = lax.axis_size("head")
    rows = queries.shape[0]
    width = saved_key_rows.shape[1]
    key_heads = width // HEAD_SIZE
    block_rows = rows * peers
    tail = block_rows // 4
    first_tail = block_rows - tail
    forward, kernels, back = spans(FORWARD), spans(KERNELS), spans(BACK)
    keys_values = (saved_key_rows, saved_value_rows, first_tail, tail)
    turns = lambda x: jnp.concatenate([turned(x, "head", by) for by in range(1, peers)])
    order = stripe_order
    early = FORWARD[:2]
    own_kv = paired(*keys_values, 0, early, (), (), ())
    peer_kv = [turns(x) for x in own_kv]
    (own_tail,) = paired(*keys_values, 0, (), (key_heads,), (order,), own_kv)
    order_before = shifted(order, "ctx", 1)
    own_tail = shifted(own_tail, "ctx", 1)
    rest_kv = paired(*keys_values, sum(early), FORWARD[2:], (), (), own_kv)
    peer_kv.append(turns(after(rest_kv[0], peer_kv[0])))
    peer_kv.append(turns(after(rest_kv[1], peer_kv[1])))
    before_kv = [shifted(x, "ctx", 1) for x in peer_kv[:2]]

    dq, outs = None, None
    terms = [None] * 3
    waiting, sent = [], []

    def send(*others):
        _, terms_first, own_terms, peer_terms, back_terms = waiting.pop(0)
        shared = peers_share(first_tail, rows, order, peer_terms, after(back_terms, dq, *others))
        shares = [
            turned(shared[(by - 1) * rows : by * rows], "head", -by) for by in range(1, peers)
        ]
        sent.append((terms_first, own_terms, back_terms, shares))
        return shared

    def total(outs):
        terms_first, own_terms, back_terms, shares = sent.pop(0)
        return total_gradients(
            order, own_terms, back_terms, shares, outs, first_tail, terms_first, width
        )

    for number, (first, count) in enumerate(kernels):
        at = next(i for i, (f, n) in enumerate(forward) if f <= first < f + n)
        if first in STARTS:
            before_kv.append(shifted(after(peer_kv[len(before_kv)], dq), "ctx", 1))
        kv_first = forward[at][0]
        terms_first, terms_count = next((f, n) for f, n in back if f <= first < f + n)
        others = [send()] if waiting and waiting[0][0] <= number - 2 else []
        dq, *terms = group_gradients(
            first_tail, order, order_before, queries, output_gradient,
            saved_output, saved_key_rows, saved_value_rows, (peer_kv[at], kv_first), (own_tail, 0),
            (before_kv[at], kv_first), first, count, dq, terms, terms_first, terms_count, others,
        )
        if first + count == terms_first + terms_count:
            own_terms, peer_terms, tail_terms = terms
            back_terms = shifted(tail_terms, "ctx", -1)
            waiting.append((number, terms_first, own_terms, peer_terms, back_terms))
            terms = [None] * 3
    while waiting:
        send()
    while sent:
        outs = total(outs)
    return (dq, *outs)


def solution(mesh):
    tokens = P(("ctx", "head"), None)
    return jax.shard_map(
        body,
        mesh=mesh,
        in_specs=(tokens, tokens, tokens, tokens, tokens, P("ctx", None)),
        out_specs=(tokens, tokens, tokens),
        check_vma=False,
    )
```

```python
import functools
import math

import jax
import jax.numpy as jnp
from jax import lax
from jax.experimental import pallas as pl
from jax.experimental.pallas import tpu as pltpu
from jax.sharding import PartitionSpec as P

HEAD_SIZE = 128
GROUP_RATIO = 4
BF16 = jnp.bfloat16
F32 = jnp.float32
VMEM_LIMIT = 23 * 2**20
SCORE_SCALE = 1.0 / math.sqrt(HEAD_SIZE)
EXP2_SCALE = SCORE_SCALE * math.log2(math.e)
HIDDEN = -1e30
PAIR = 2 * HEAD_SIZE
POS_ROWS = 16
SHORT = pl.CostEstimate(flops=1, bytes_accessed=1, transcendentals=0)

NT = (((1,), (1,)), ((), ()))
NN = (((1,), (0,)), ((), ()))


def dot(a, b, dims=NN):
    return lax.dot_general(a, b, dims, preferred_element_type=F32)


def params():
    return pltpu.CompilerParams(vmem_limit_bytes=VMEM_LIMIT)


def key_tile(keys):
    return next(size for size in (640, 256, 128) if keys % size == 0)


def positions(order, rows):
    me, peers = lax.axis_index("head"), lax.axis_size("head")
    at = [lax.rem(me + peers - by, peers) * rows for by in range(peers)]
    parts = [order[:, pl.ds(pl.multiple_of(x, 128), rows)] for x in at]
    return parts[0], jnp.concatenate(parts[1:], axis=1)


def coded(pos):
    row = lax.broadcasted_iota(jnp.int32, (POS_ROWS, pos.shape[1]), 0)
    digits = jnp.where(row == 0, pos >> 5, jnp.where(row == 1, pos & 31, 0))
    return digits.astype(F32).astype(BF16)


def decoded(rows):
    rows = rows.astype(F32)
    return (rows[0:1] * 32.0 + rows[1:2]).astype(jnp.int32)


def one_hot(pos, first, tail):
    wanted = first + lax.broadcasted_iota(jnp.int32, (tail, pos.shape[1]), 0)
    return (pos == wanted).astype(BF16)


def pair_kernel(first_tail, start, sizes, tails, keys, values, *refs):
    outs = refs[-len(sizes + tails) :]
    heads = [(out, at) for out, size in zip(outs, sizes) for at in range(size)]
    for head, (out, at) in enumerate(heads, start):
        columns = slice(head * HEAD_SIZE, (head + 1) * HEAD_SIZE)
        out[:, at * PAIR : at * PAIR + HEAD_SIZE] = keys[:, columns]
        out[:, at * PAIR + HEAD_SIZE : (at + 1) * PAIR] = values[:, columns]
    if tails:
        own_pos, peer_pos = positions(refs[0], keys.shape[0])
        picks = one_hot(own_pos, first_tail, outs[-1].shape[0] - POS_ROWS)
        heads = [(out, at) for out, size in zip(outs[len(sizes) :], tails) for at in range(size)]
        for head, (out, at) in enumerate(heads):
            columns = slice(head * HEAD_SIZE, (head + 1) * HEAD_SIZE)
            for side, x in enumerate((keys, values)):
                lane = at * PAIR + side * HEAD_SIZE
                out[: -POS_ROWS, lane : lane + HEAD_SIZE] = dot(picks, x[:, columns]).astype(BF16)
        for out in outs[len(sizes) :]:
            out[-POS_ROWS:, : peer_pos.shape[1]] = coded(peer_pos)


def copy_kernel(sizes, keys, values, *refs):
    outs, sem = refs[:-1], refs[-1]
    heads = [(out, at) for out, size in zip(outs, sizes) for at in range(size)]
    copies = []
    for head, (out, at) in enumerate(heads):
        for side, x in enumerate((keys, values)):
            lane = at * PAIR + side * HEAD_SIZE
            copies.append(
                pltpu.make_async_copy(
                    x.at[:, head * HEAD_SIZE : (head + 1) * HEAD_SIZE],
                    out.at[:, lane : lane + HEAD_SIZE],
                    sem.at[len(copies)],
                )
            )
            copies[-1].start()
    for copy in copies:
        copy.wait()


def paired_first(keys, values, sizes):
    rows = keys.shape[0]
    hbm = pl.BlockSpec(memory_space=pltpu.HBM)
    return pl.pallas_call(
        functools.partial(copy_kernel, sizes),
        in_specs=[hbm, hbm],
        out_specs=[hbm for _ in sizes],
        out_shape=[jax.ShapeDtypeStruct((rows, n * PAIR), BF16) for n in sizes],
        scratch_shapes=[pltpu.SemaphoreType.DMA((2 * sum(sizes),))],
        compiler_params=params(),
        cost_estimate=SHORT,
        name="paired_first",
    )(keys, values)


def paired(keys, values, first_tail, tail, start, sizes, tails, pos, others):
    rows, width = keys.shape
    shapes = [(rows, n * PAIR) for n in sizes] + [(tail + POS_ROWS, n * PAIR) for n in tails]
    used = max(start + sum(sizes), sum(tails)) * HEAD_SIZE
    block = pl.BlockSpec((rows, used), lambda i: (0, 0))
    whole = lambda x: pl.BlockSpec(x.shape, lambda i: (0, 0))
    shapes = [jax.ShapeDtypeStruct(shape, BF16) for shape in shapes]
    return pl.pallas_call(
        functools.partial(pair_kernel, first_tail, start, sizes, tails),
        grid=(1,),
        in_specs=[block, block, *map(whole, pos)]
        + [pl.BlockSpec(memory_space=pl.ANY)] * len(others),
        out_specs=[whole(x) for x in shapes],
        out_shape=shapes,
        compiler_params=params(),
        cost_estimate=SHORT,
        name="paired",
    )(keys, values, *pos, *others)


def group_kernel(
    first_tail, order, code_before, queries, grads, outputs, own_k, own_v, peer_kv, own_tail,
    before_kv, *rest
):
    (k_all, kt_all, v_all, bias, dk, dv) = rest[-12:-6]
    delta = {}
    scores, probs, dscores = rest[-6:-4], rest[-4:-2], rest[-2:]
    (dq, own_terms, peer_terms, tail_terms) = rest[-16:-12]
    rows = queries.shape[0]
    keys = k_all.shape[0]
    own, peer = own_k.shape[0], peer_kv.shape[0]
    query_tile = min(256, rows)
    query_tiles = rows // query_tile
    steps = queries.shape[1] // HEAD_SIZE * query_tiles
    tile = key_tile(keys)
    blocks = [slice(at, at + tile) for at in range(0, keys, tile)]

    @pl.when(pl.program_id(0) == 0)
    def _():
        query_pos, peer_pos = positions(order, rows)
        late_pos = jnp.where(lax.axis_index("ctx") > 0, -1, own + peer)
        late_pos = jnp.full((1, own_tail.shape[0]), late_pos, jnp.int32)
        key_pos = jnp.concatenate([query_pos, peer_pos, late_pos], axis=1).astype(F32)
        column = jnp.broadcast_to(key_pos, (8, keys)).T[:, :1]
        bias[...] = jnp.where(column <= query_pos.astype(F32), 0.0, HIDDEN)

    for whole, mine, side in ((k_all, own_k, 0), (v_all, own_v, HEAD_SIZE)):
        whole[:own] = mine[...]
        whole[own : own + peer] = peer_kv[:, side : side + HEAD_SIZE]
    tail = own_tail.shape[0]
    before_pos = decoded(code_before[...])
    late = own_tail[...].astype(F32) + dot(one_hot(before_pos, first_tail, tail), before_kv[...])
    k_all[own + peer :] = late[:, :HEAD_SIZE].astype(BF16)
    v_all[own + peer :] = late[:, HEAD_SIZE:].astype(BF16)
    kt_all[...] = k_all[...].astype(F32).T.astype(BF16)
    top, inverse_sum = {}, {}

    def place(step):
        head, at = divmod(step, query_tiles)
        return (
            slice(at * query_tile, (at + 1) * query_tile),
            slice(head * HEAD_SIZE, (head + 1) * HEAD_SIZE),
        )

    def fold(x):
        return x.reshape(tile // 8, 8, query_tile)

    def score_block(step, block):
        at, columns = place(step)
        s = dot(k_all[block], queries[at, columns], NT) * EXP2_SCALE + bias[block, at]
        scores[step % 2][block] = s
        high = jnp.max(fold(s), axis=0)
        top[step] = jnp.maximum(top[step], high) if step in top else high

    def delta_row(step):
        at, columns = place(step)
        product = outputs[at, columns].astype(F32) * grads[at, columns].astype(F32)
        delta[step] = jnp.sum(product.T, axis=0, keepdims=True)

    def exp_block(step, block):
        e = jnp.exp2(scores[step % 2][block] - top[step])
        scores[step % 2][block] = e
        total = jnp.sum(fold(e), axis=0)
        inverse_sum[step] = inverse_sum[step] + total if step in inverse_sum else total

    def dscore_block(step, block):
        at, columns = place(step)
        p = scores[step % 2][block] * inverse_sum[step]
        dprob = dot(v_all[block], grads[at, columns], NT)
        probs[step % 2][block] = p.astype(BF16)
        dscores[step % 2][block] = (p * (dprob - delta[step])).astype(BF16)

    def key_block(step, block):
        at, columns = place(step)
        value_term = dot(probs[step % 2][block], grads[at, columns])
        key_term = dot(dscores[step % 2][block], queries[at, columns])
        if step == 0:
            dv[block] = value_term
            dk[block] = key_term
        else:
            dv[block] += value_term
            dk[block] += key_term

    for block in blocks:
        score_block(0, block)
    for step in range(steps + 1):
        if step < steps:
            top[step] = jnp.max(top[step], axis=0, keepdims=True)
            delta_row(step)
        for block in blocks:
            if step < steps:
                exp_block(step, block)
            if step > 0:
                key_block(step - 1, block)
        if step > 0:
            at, columns = place(step - 1)
            dq_t = dot(kt_all[...], dscores[(step - 1) % 2][...])
            dq[at, columns] = (dq_t * SCORE_SCALE).T.astype(BF16)
        if step < steps:
            inverse_sum[step] = 1.0 / jnp.sum(inverse_sum[step], axis=0, keepdims=True)
        for block in blocks:
            if step + 1 < steps:
                score_block(step + 1, block)
            if step < steps:
                dscore_block(step, block)

    for whole, side, scale in ((dk, 0, SCORE_SCALE), (dv, HEAD_SIZE, 1.0)):
        columns = slice(side, side + HEAD_SIZE)
        own_terms[:, columns] = whole[:own] * scale
        peer_terms[:, columns] = whole[own : own + peer] * scale
        tail_terms[:, columns] = (whole[own + peer :] * scale).astype(BF16)


def group_gradients(
    first_tail, order, queries, grads, outputs, keys, values, peer_kv,
    own_tail, before_kv, first, count, dq, terms, terms_first, terms_count, others,
):
    rows, width = queries.shape
    (peer_kv, peer_first), (own_tail, tail_first), (before_kv, before_first) = (
        peer_kv, own_tail, before_kv
    )
    peer, tail = peer_kv.shape[0], own_tail.shape[0] - POS_ROWS
    total = rows + peer + tail
    group = GROUP_RATIO * HEAD_SIZE
    query_tile = min(256, rows)
    query_spec = pl.BlockSpec((rows, group), lambda g: (0, first + g))
    own_spec = pl.BlockSpec((rows, HEAD_SIZE), lambda g: (0, first + g))

    def pair_spec(n, start):
        return pl.BlockSpec((n, PAIR), lambda g: (0, first - start + g))

    whole = lambda x: pl.BlockSpec(x.shape, lambda g: (0, 0))
    in_specs = [
        whole(order),
        pl.BlockSpec((POS_ROWS, peer), lambda g: (tail // POS_ROWS, 0)),
        query_spec,
        query_spec,
        query_spec,
        own_spec,
        own_spec,
        pair_spec(peer, peer_first),
        pair_spec(tail, tail_first),
        pair_spec(peer, before_first),
    ]
    operands = [
        order, own_tail, queries, grads, outputs, keys, values, peer_kv, own_tail, before_kv,
    ]
    out_specs = [query_spec] + [pair_spec(n, terms_first) for n in (rows, peer, tail)]
    out_shape = [
        jax.ShapeDtypeStruct((rows, width), BF16),
        jax.ShapeDtypeStruct((rows, terms_count * PAIR), F32),
        jax.ShapeDtypeStruct((peer, terms_count * PAIR), F32),
        jax.ShapeDtypeStruct((tail, terms_count * PAIR), BF16),
    ]
    aliases = {}
    for at, buffer in enumerate((dq, *terms)):
        if buffer is not None:
            aliases[len(operands)] = at
            operands.append(buffer)
    operands += others
    in_specs += [pl.BlockSpec(memory_space=pl.ANY)] * (len(operands) - len(in_specs))
    pairs = total * rows * GROUP_RATIO * count
    return pl.pallas_call(
        functools.partial(group_kernel, first_tail),
        grid=(count,),
        in_specs=in_specs,
        out_specs=out_specs,
        out_shape=out_shape,
        scratch_shapes=[
            pltpu.VMEM((total, HEAD_SIZE), BF16),
            pltpu.VMEM((HEAD_SIZE, total), BF16),
            pltpu.VMEM((total, HEAD_SIZE), BF16),
            pltpu.VMEM((total, rows), F32),
            pltpu.VMEM((total, HEAD_SIZE), F32),
            pltpu.VMEM((total, HEAD_SIZE), F32),
            *[pltpu.VMEM((total, query_tile), F32)] * 2,
            *[pltpu.VMEM((total, query_tile), BF16)] * 4,
        ],
        input_output_aliases=aliases,
        compiler_params=params(),
        cost_estimate=pl.CostEstimate(
            flops=20 * pairs * HEAD_SIZE,
            bytes_accessed=6 * rows * group * count,
            transcendentals=pairs,
        ),
        name="group_gradients",
    )(*operands)


def spread(first, pos, terms):
    picks = one_hot(pos, first, terms.shape[0]).astype(F32).T.astype(BF16)
    return dot(picks, terms[...])


def share_kernel(first, rows, order, peer_terms, back, shared):
    _, pos = positions(order, rows)
    shared[...] = (peer_terms[...] + spread(first, pos, back)).astype(BF16)


def peers_share(first, rows, order, peer_terms, back):
    return pl.pallas_call(
        functools.partial(share_kernel, first, rows),
        out_shape=jax.ShapeDtypeStruct(peer_terms.shape, BF16),
        compiler_params=params(),
        cost_estimate=SHORT,
        name="peers_share",
    )(order, peer_terms, back)


def total_kernel(first, peers, order, own_terms, back, *rest):
    shares, (key_grad, value_grad) = rest[: peers - 1], rest[-2:]
    pos, _ = positions(order, own_terms.shape[0])
    total = own_terms[...] + spread(first, pos, back)
    for share in shares:
        total += share[...].astype(F32)
    for at in range(total.shape[1] // PAIR):
        columns = slice(at * HEAD_SIZE, (at + 1) * HEAD_SIZE)
        key_grad[:, columns] = total[:, at * PAIR : at * PAIR + HEAD_SIZE].astype(BF16)
        value_grad[:, columns] = total[:, at * PAIR + HEAD_SIZE : (at + 1) * PAIR].astype(BF16)


def total_gradients(order, own_terms, back, shares, outs, first_tail, first, width):
    rows, part = own_terms.shape
    count = part // PAIR
    step = count if first % count == 0 else 1
    one = lambda x: pl.BlockSpec((x.shape[0], step * PAIR), lambda g: (0, g))
    operands = [order, own_terms, back, *shares]
    in_specs = [pl.BlockSpec(order.shape, lambda g: (0, 0)), *map(one, operands[1:])]
    aliases = {}
    if outs is not None:
        aliases = {len(operands): 0, len(operands) + 1: 1}
        operands += outs
        in_specs += [pl.BlockSpec(memory_space=pl.ANY)] * 2
    out = pl.BlockSpec((rows, step * HEAD_SIZE), lambda g: (0, first // step + g))
    return pl.pallas_call(
        functools.partial(total_kernel, first_tail, len(shares) + 1),
        grid=(count // step,),
        in_specs=in_specs,
        out_specs=[out, out],
        out_shape=[jax.ShapeDtypeStruct((rows, width), BF16)] * 2,
        input_output_aliases=aliases,
        compiler_params=params(),
        cost_estimate=SHORT,
        name="total_gradients",
    )(*operands)


def shifted(x, axis, by):
    peers = lax.axis_size(axis)
    pairs = [(i, i + by) for i in range(peers) if 0 <= i + by < peers]
    return lax.ppermute(x, axis, pairs)


def turned(x, axis, by):
    peers = lax.axis_size(axis)
    return lax.ppermute(x, axis, [(i, (i + by) % peers) for i in range(peers)])


def spans(sizes):
    return [(sum(sizes[:i]), size) for i, size in enumerate(sizes)]


def after(x, *others):
    return lax.optimization_barrier((x, *others))[0]


FORWARD = (1, 1, 2, 4)
KERNELS = (1, 1, 1, 1, 2, 1, 1)
BACK = (4, 2, 2)
STARTS = (1, 3)


def body(queries, saved_key_rows, saved_value_rows, saved_output, output_gradient, stripe_order):
    peers = lax.axis_size("head")
    rows = queries.shape[0]
    width = saved_key_rows.shape[1]
    key_heads = width // HEAD_SIZE
    block_rows = rows * peers
    tail = block_rows // 4
    first_tail = block_rows - tail
    forward, kernels, back = spans(FORWARD), spans(KERNELS), spans(BACK)
    keys_values = (saved_key_rows, saved_value_rows, first_tail, tail)
    turns = lambda x: jnp.concatenate([turned(x, "head", by) for by in range(1, peers)])
    order = stripe_order
    early = FORWARD[:2]
    own_kv = paired_first(saved_key_rows, saved_value_rows, early)
    peer_kv = [turns(x) for x in own_kv]
    (own_tail,) = paired(*keys_values, 0, (), (key_heads,), (order,), own_kv)
    own_tail = shifted(own_tail, "ctx", 1)
    rest_kv = paired(*keys_values, sum(early), FORWARD[2:], (), (), own_kv)
    peer_kv.append(turns(after(rest_kv[0], peer_kv[0])))
    peer_kv.append(turns(after(rest_kv[1], peer_kv[1])))
    before_kv = [shifted(x, "ctx", 1) for x in peer_kv[:2]]

    dq, outs = None, None
    terms = [None] * 3
    waiting, sent = [], []

    def send(*others):
        _, terms_first, own_terms, peer_terms, back_terms = waiting.pop(0)
        shared = peers_share(first_tail, rows, order, peer_terms, after(back_terms, dq, *others))
        shares = [
            turned(shared[(by - 1) * rows : by * rows], "head", -by) for by in range(1, peers)
        ]
        sent.append((terms_first, own_terms, back_terms, shares))
        return shared

    def total(outs):
        terms_first, own_terms, back_terms, shares = sent.pop(0)
        return total_gradients(
            order, own_terms, back_terms, shares, outs, first_tail, terms_first, width
        )

    for number, (first, count) in enumerate(kernels):
        at = next(i for i, (f, n) in enumerate(forward) if f <= first < f + n)
        if first in STARTS:
            before_kv.append(shifted(after(peer_kv[len(before_kv)], dq), "ctx", 1))
        kv_first = forward[at][0]
        terms_first, terms_count = next((f, n) for f, n in back if f <= first < f + n)
        others = [send()] if waiting and waiting[0][0] <= number - 2 else []
        dq, *terms = group_gradients(
            first_tail, order, queries, output_gradient,
            saved_output, saved_key_rows, saved_value_rows, (peer_kv[at], kv_first), (own_tail, 0),
            (before_kv[at], kv_first), first, count, dq, terms, terms_first, terms_count, others,
        )
        if first + count == terms_first + terms_count:
            own_terms, peer_terms, tail_terms = terms
            back_terms = shifted(tail_terms, "ctx", -1)
            waiting.append((number, terms_first, own_terms, peer_terms, back_terms))
            terms = [None] * 3
    while waiting:
        send()
    while sent:
        outs = total(outs)
    return (dq, *outs)


def solution(mesh):
    tokens = P(("ctx", "head"), None)
    return jax.shard_map(
        body,
        mesh=mesh,
        in_specs=(tokens, tokens, tokens, tokens, tokens, P("ctx", None)),
        out_specs=(tokens, tokens, tokens),
        check_vma=False,
    )
```

```python
import functools
import math

import jax
import jax.numpy as jnp
from jax import lax
from jax.experimental import pallas as pl
from jax.experimental.pallas import tpu as pltpu
from jax.sharding import PartitionSpec as P

HEAD_SIZE = 128
GROUP_RATIO = 4
BF16 = jnp.bfloat16
F32 = jnp.float32
VMEM_LIMIT = 23 * 2**20
SCORE_SCALE = 1.0 / math.sqrt(HEAD_SIZE)
EXP2_SCALE = SCORE_SCALE * math.log2(math.e)
HIDDEN = -1e30
PAIR = 2 * HEAD_SIZE
POS_ROWS = 16
SHORT = pl.CostEstimate(flops=1, bytes_accessed=1, transcendentals=0)

NT = (((1,), (1,)), ((), ()))
NN = (((1,), (0,)), ((), ()))


def dot(a, b, dims=NN):
    return lax.dot_general(a, b, dims, preferred_element_type=F32)


def params():
    return pltpu.CompilerParams(vmem_limit_bytes=VMEM_LIMIT)


def key_tile(keys):
    return next(size for size in (640, 256, 128) if keys % size == 0)


def positions(order, rows):
    me, peers = lax.axis_index("head"), lax.axis_size("head")
    at = [lax.rem(me + peers - by, peers) * rows for by in range(peers)]
    parts = [order[:, pl.ds(pl.multiple_of(x, 128), rows)] for x in at]
    return parts[0], jnp.concatenate(parts[1:], axis=1)


def coded(pos):
    row = lax.broadcasted_iota(jnp.int32, (POS_ROWS, pos.shape[1]), 0)
    digits = jnp.where(row == 0, pos >> 5, jnp.where(row == 1, pos & 31, 0))
    return digits.astype(F32).astype(BF16)


def decoded(rows):
    rows = rows.astype(F32)
    return (rows[0:1] * 32.0 + rows[1:2]).astype(jnp.int32)


def one_hot(pos, first, tail):
    wanted = first + lax.broadcasted_iota(jnp.int32, (tail, pos.shape[1]), 0)
    return (pos == wanted).astype(BF16)


def pair_kernel(first_tail, start, sizes, tails, keys, values, *refs):
    outs = refs[-len(sizes + tails) :]
    heads = [(out, at) for out, size in zip(outs, sizes) for at in range(size)]
    for head, (out, at) in enumerate(heads, start):
        columns = slice(head * HEAD_SIZE, (head + 1) * HEAD_SIZE)
        out[:, at * PAIR : at * PAIR + HEAD_SIZE] = keys[:, columns]
        out[:, at * PAIR + HEAD_SIZE : (at + 1) * PAIR] = values[:, columns]
    if tails:
        own_pos, peer_pos = positions(refs[0], keys.shape[0])
        picks = one_hot(own_pos, first_tail, outs[-1].shape[0] - POS_ROWS)
        heads = [(out, at) for out, size in zip(outs[len(sizes) :], tails) for at in range(size)]
        for head, (out, at) in enumerate(heads):
            columns = slice(head * HEAD_SIZE, (head + 1) * HEAD_SIZE)
            for side, x in enumerate((keys, values)):
                lane = at * PAIR + side * HEAD_SIZE
                out[: -POS_ROWS, lane : lane + HEAD_SIZE] = dot(picks, x[:, columns]).astype(BF16)
        for out in outs[len(sizes) :]:
            out[-POS_ROWS:, : peer_pos.shape[1]] = coded(peer_pos)


def copy_kernel(sizes, keys, values, *refs):
    outs, sem = refs[:-1], refs[-1]
    heads = [(out, at) for out, size in zip(outs, sizes) for at in range(size)]
    copies = []
    for head, (out, at) in enumerate(heads):
        for side, x in enumerate((keys, values)):
            lane = at * PAIR + side * HEAD_SIZE
            copies.append(
                pltpu.make_async_copy(
                    x.at[:, head * HEAD_SIZE : (head + 1) * HEAD_SIZE],
                    out.at[:, lane : lane + HEAD_SIZE],
                    sem.at[len(copies)],
                )
            )
            copies[-1].start()
    for copy in copies:
        copy.wait()


def paired_first(keys, values, sizes):
    rows = keys.shape[0]
    hbm = pl.BlockSpec(memory_space=pltpu.HBM)
    return pl.pallas_call(
        functools.partial(copy_kernel, sizes),
        in_specs=[hbm, hbm],
        out_specs=[hbm for _ in sizes],
        out_shape=[jax.ShapeDtypeStruct((rows, n * PAIR), BF16) for n in sizes],
        scratch_shapes=[pltpu.SemaphoreType.DMA((2 * sum(sizes),))],
        compiler_params=params(),
        cost_estimate=SHORT,
        name="paired_first",
    )(keys, values)


def paired(keys, values, first_tail, tail, start, sizes, tails, pos, others):
    rows, width = keys.shape
    shapes = [(rows, n * PAIR) for n in sizes] + [(tail + POS_ROWS, n * PAIR) for n in tails]
    used = max(start + sum(sizes), sum(tails)) * HEAD_SIZE
    block = pl.BlockSpec((rows, used), lambda i: (0, 0))
    whole = lambda x: pl.BlockSpec(x.shape, lambda i: (0, 0))
    shapes = [jax.ShapeDtypeStruct(shape, BF16) for shape in shapes]
    return pl.pallas_call(
        functools.partial(pair_kernel, first_tail, start, sizes, tails),
        grid=(1,),
        in_specs=[block, block, *map(whole, pos)]
        + [pl.BlockSpec(memory_space=pl.ANY)] * len(others),
        out_specs=[whole(x) for x in shapes],
        out_shape=shapes,
        compiler_params=params(),
        cost_estimate=SHORT,
        name="paired",
    )(keys, values, *pos, *others)


def group_kernel(
    first_tail, order, code_before, queries, grads, outputs, own_k, own_v, peer_kv, own_tail,
    before_kv, *rest
):
    (k_all, kt_all, v_all, bias, dk, dv) = rest[-12:-6]
    delta = {}
    scores, probs, dscores = rest[-6:-4], rest[-4:-2], rest[-2:]
    (dq, own_terms, peer_terms, tail_terms) = rest[-16:-12]
    rows = queries.shape[0]
    keys = k_all.shape[0]
    own, peer = own_k.shape[0], peer_kv.shape[0]
    query_tile = min(256, rows)
    query_tiles = rows // query_tile
    steps = queries.shape[1] // HEAD_SIZE * query_tiles
    tile = key_tile(keys)
    blocks = [slice(at, at + tile) for at in range(0, keys, tile)]

    @pl.when(pl.program_id(0) == 0)
    def _():
        query_pos, peer_pos = positions(order, rows)
        late_pos = jnp.where(lax.axis_index("ctx") > 0, -1, own + peer)
        late_pos = jnp.full((1, own_tail.shape[0]), late_pos, jnp.int32)
        key_pos = jnp.concatenate([query_pos, peer_pos, late_pos], axis=1).astype(F32)
        column = jnp.broadcast_to(key_pos, (8, keys)).T[:, :1]
        bias[...] = jnp.where(column <= query_pos.astype(F32), 0.0, HIDDEN)

    for whole, mine, side in ((k_all, own_k, 0), (v_all, own_v, HEAD_SIZE)):
        whole[:own] = mine[...]
        whole[own : own + peer] = peer_kv[:, side : side + HEAD_SIZE]
    tail = own_tail.shape[0]
    before_pos = decoded(code_before[...])
    late = own_tail[...].astype(F32) + dot(one_hot(before_pos, first_tail, tail), before_kv[...])
    k_all[own + peer :] = late[:, :HEAD_SIZE].astype(BF16)
    v_all[own + peer :] = late[:, HEAD_SIZE:].astype(BF16)
    kt_all[...] = k_all[...].astype(F32).T.astype(BF16)
    top, inverse_sum = {}, {}

    def place(step):
        head, at = divmod(step, query_tiles)
        return (
            slice(at * query_tile, (at + 1) * query_tile),
            slice(head * HEAD_SIZE, (head + 1) * HEAD_SIZE),
        )

    def fold(x):
        return x.reshape(tile // 8, 8, query_tile)

    def score_block(step, block):
        at, columns = place(step)
        s = dot(k_all[block], queries[at, columns], NT) * EXP2_SCALE + bias[block, at]
        scores[step % 2][block] = s
        high = jnp.max(fold(s), axis=0)
        top[step] = jnp.maximum(top[step], high) if step in top else high

    def delta_row(step):
        at, columns = place(step)
        product = outputs[at, columns].astype(F32) * grads[at, columns].astype(F32)
        delta[step] = jnp.sum(product.T, axis=0, keepdims=True)

    def exp_block(step, block):
        e = jnp.exp2(scores[step % 2][block] - top[step])
        scores[step % 2][block] = e
        total = jnp.sum(fold(e), axis=0)
        inverse_sum[step] = inverse_sum[step] + total if step in inverse_sum else total

    def dscore_block(step, block):
        at, columns = place(step)
        p = scores[step % 2][block] * inverse_sum[step]
        dprob = dot(v_all[block], grads[at, columns], NT)
        probs[step % 2][block] = p.astype(BF16)
        dscores[step % 2][block] = (p * (dprob - delta[step])).astype(BF16)

    def key_block(step, block):
        at, columns = place(step)
        value_term = dot(probs[step % 2][block], grads[at, columns])
        key_term = dot(dscores[step % 2][block], queries[at, columns])
        if step == 0:
            dv[block] = value_term
            dk[block] = key_term
        else:
            dv[block] += value_term
            dk[block] += key_term

    for block in blocks:
        score_block(0, block)
    for step in range(steps + 1):
        if step < steps:
            top[step] = jnp.max(top[step], axis=0, keepdims=True)
            delta_row(step)
        for block in blocks:
            if step < steps:
                exp_block(step, block)
            if step > 0:
                key_block(step - 1, block)
        if step > 0:
            at, columns = place(step - 1)
            dq_t = dot(kt_all[...], dscores[(step - 1) % 2][...])
            dq[at, columns] = (dq_t * SCORE_SCALE).T.astype(BF16)
        if step < steps:
            inverse_sum[step] = 1.0 / jnp.sum(inverse_sum[step], axis=0, keepdims=True)
        for block in blocks:
            if step + 1 < steps:
                score_block(step + 1, block)
            if step < steps:
                dscore_block(step, block)

    for whole, side, scale in ((dk, 0, SCORE_SCALE), (dv, HEAD_SIZE, 1.0)):
        columns = slice(side, side + HEAD_SIZE)
        own_terms[:, columns] = whole[:own] * scale
        peer_terms[:, columns] = whole[own : own + peer] * scale
        tail_terms[:, columns] = (whole[own + peer :] * scale).astype(BF16)


def group_gradients(
    first_tail, order, queries, grads, outputs, keys, values, peer_kv,
    own_tail, before_kv, first, count, dq, terms, terms_first, terms_count, others,
):
    rows, width = queries.shape
    (peer_kv, peer_first), (own_tail, tail_first), (before_kv, before_first) = (
        peer_kv, own_tail, before_kv
    )
    peer, tail = peer_kv.shape[0], own_tail.shape[0] - POS_ROWS
    total = rows + peer + tail
    group = GROUP_RATIO * HEAD_SIZE
    query_tile = min(256, rows)
    query_spec = pl.BlockSpec((rows, group), lambda g: (0, first + g))
    own_spec = pl.BlockSpec((rows, HEAD_SIZE), lambda g: (0, first + g))

    def pair_spec(n, start):
        return pl.BlockSpec((n, PAIR), lambda g: (0, first - start + g))

    whole = lambda x: pl.BlockSpec(x.shape, lambda g: (0, 0))
    in_specs = [
        whole(order),
        pl.BlockSpec((POS_ROWS, peer), lambda g: (tail // POS_ROWS, 0)),
        query_spec,
        query_spec,
        query_spec,
        own_spec,
        own_spec,
        pair_spec(peer, peer_first),
        pair_spec(tail, tail_first),
        pair_spec(peer, before_first),
    ]
    operands = [
        order, own_tail, queries, grads, outputs, keys, values, peer_kv, own_tail, before_kv,
    ]
    out_specs = [query_spec] + [pair_spec(n, terms_first) for n in (rows, peer, tail)]
    out_shape = [
        jax.ShapeDtypeStruct((rows, width), BF16),
        jax.ShapeDtypeStruct((rows, terms_count * PAIR), F32),
        jax.ShapeDtypeStruct((peer, terms_count * PAIR), F32),
        jax.ShapeDtypeStruct((tail, terms_count * PAIR), BF16),
    ]
    aliases = {}
    for at, buffer in enumerate((dq, *terms)):
        if buffer is not None:
            aliases[len(operands)] = at
            operands.append(buffer)
    operands += others
    in_specs += [pl.BlockSpec(memory_space=pl.ANY)] * (len(operands) - len(in_specs))
    pairs = total * rows * GROUP_RATIO * count
    return pl.pallas_call(
        functools.partial(group_kernel, first_tail),
        grid=(count,),
        in_specs=in_specs,
        out_specs=out_specs,
        out_shape=out_shape,
        scratch_shapes=[
            pltpu.VMEM((total, HEAD_SIZE), BF16),
            pltpu.VMEM((HEAD_SIZE, total), BF16),
            pltpu.VMEM((total, HEAD_SIZE), BF16),
            pltpu.VMEM((total, rows), F32),
            pltpu.VMEM((total, HEAD_SIZE), F32),
            pltpu.VMEM((total, HEAD_SIZE), F32),
            *[pltpu.VMEM((total, query_tile), F32)] * 2,
            *[pltpu.VMEM((total, query_tile), BF16)] * 4,
        ],
        input_output_aliases=aliases,
        compiler_params=params(),
        cost_estimate=pl.CostEstimate(
            flops=20 * pairs * HEAD_SIZE,
            bytes_accessed=6 * rows * group * count,
            transcendentals=pairs,
        ),
        name="group_gradients",
    )(*operands)


def spread(first, pos, terms):
    picks = one_hot(pos, first, terms.shape[0]).astype(F32).T.astype(BF16)
    return dot(picks, terms[...])


def share_kernel(first, rows, order, peer_terms, back, shared):
    _, pos = positions(order, rows)
    shared[...] = (peer_terms[...] + spread(first, pos, back)).astype(BF16)


def peers_share(first, rows, order, peer_terms, back):
    return pl.pallas_call(
        functools.partial(share_kernel, first, rows),
        out_shape=jax.ShapeDtypeStruct(peer_terms.shape, BF16),
        compiler_params=params(),
        cost_estimate=SHORT,
        name="peers_share",
    )(order, peer_terms, back)


def total_kernel(first, peers, order, own_terms, back, *rest):
    shares, (key_grad, value_grad) = rest[: peers - 1], rest[-2:]
    pos, _ = positions(order, own_terms.shape[0])
    total = own_terms[...] + spread(first, pos, back)
    for share in shares:
        total += share[...].astype(F32)
    for at in range(total.shape[1] // PAIR):
        columns = slice(at * HEAD_SIZE, (at + 1) * HEAD_SIZE)
        key_grad[:, columns] = total[:, at * PAIR : at * PAIR + HEAD_SIZE].astype(BF16)
        value_grad[:, columns] = total[:, at * PAIR + HEAD_SIZE : (at + 1) * PAIR].astype(BF16)


def total_gradients(order, own_terms, back, shares, outs, first_tail, first, width):
    rows, part = own_terms.shape
    count = part // PAIR
    step = count if first % count == 0 else 1
    one = lambda x: pl.BlockSpec((x.shape[0], step * PAIR), lambda g: (0, g))
    operands = [order, own_terms, back, *shares]
    in_specs = [pl.BlockSpec(order.shape, lambda g: (0, 0)), *map(one, operands[1:])]
    aliases = {}
    if outs is not None:
        aliases = {len(operands): 0, len(operands) + 1: 1}
        operands += outs
        in_specs += [pl.BlockSpec(memory_space=pl.ANY)] * 2
    out = pl.BlockSpec((rows, step * HEAD_SIZE), lambda g: (0, first // step + g))
    return pl.pallas_call(
        functools.partial(total_kernel, first_tail, len(shares) + 1),
        grid=(count // step,),
        in_specs=in_specs,
        out_specs=[out, out],
        out_shape=[jax.ShapeDtypeStruct((rows, width), BF16)] * 2,
        input_output_aliases=aliases,
        compiler_params=params(),
        cost_estimate=SHORT,
        name="total_gradients",
    )(*operands)


def shifted(x, axis, by):
    peers = lax.axis_size(axis)
    pairs = [(i, i + by) for i in range(peers) if 0 <= i + by < peers]
    return lax.ppermute(x, axis, pairs)


def turned(x, axis, by):
    peers = lax.axis_size(axis)
    return lax.ppermute(x, axis, [(i, (i + by) % peers) for i in range(peers)])


def spans(sizes):
    return [(sum(sizes[:i]), size) for i, size in enumerate(sizes)]


def after(x, *others):
    return lax.optimization_barrier((x, *others))[0]


FORWARD = (1, 1, 2, 4)
KERNELS = (1,) * 8
BACK = (4, 2, 1, 1)
LATE = 1
STARTS = (1, 3)


def body(queries, saved_key_rows, saved_value_rows, saved_output, output_gradient, stripe_order):
    peers = lax.axis_size("head")
    rows = queries.shape[0]
    width = saved_key_rows.shape[1]
    key_heads = width // HEAD_SIZE
    block_rows = rows * peers
    tail = block_rows // 4
    first_tail = block_rows - tail
    forward, kernels, back = spans(FORWARD), spans(KERNELS), spans(BACK)
    keys_values = (saved_key_rows, saved_value_rows, first_tail, tail)
    turns = lambda x: jnp.concatenate([turned(x, "head", by) for by in range(1, peers)])
    order = stripe_order
    early = FORWARD[:2]
    own_kv = paired_first(saved_key_rows, saved_value_rows, early)
    peer_kv = [turns(x) for x in own_kv]
    (own_tail,) = paired(*keys_values, 0, (), (key_heads,), (order,), own_kv)
    own_tail = shifted(own_tail, "ctx", 1)
    rest_kv = paired(*keys_values, sum(early), FORWARD[2:], (), (), own_kv)
    peer_kv.append(turns(after(rest_kv[0], peer_kv[0])))
    peer_kv.append(turns(after(rest_kv[1], peer_kv[1])))
    before_kv = [shifted(x, "ctx", 1) for x in peer_kv[:2]]

    dq, outs = None, None
    terms = [None] * 3
    waiting, sent = [], []

    def send(*others):
        _, terms_first, own_terms, peer_terms, back_terms = waiting.pop(0)
        shared = peers_share(first_tail, rows, order, peer_terms, after(back_terms, dq, *others))
        shares = [
            turned(shared[(by - 1) * rows : by * rows], "head", -by) for by in range(1, peers)
        ]
        sent.append((terms_first, own_terms, back_terms, shares))
        return shared

    def total(outs):
        terms_first, own_terms, back_terms, shares = sent.pop(0)
        return total_gradients(
            order, own_terms, back_terms, shares, outs, first_tail, terms_first, width
        )

    for number, (first, count) in enumerate(kernels):
        at = next(i for i, (f, n) in enumerate(forward) if f <= first < f + n)
        if first in STARTS:
            before_kv.append(shifted(after(peer_kv[len(before_kv)], dq), "ctx", 1))
        kv_first = forward[at][0]
        terms_first, terms_count = next((f, n) for f, n in back if f <= first < f + n)
        others = [send()] if waiting and waiting[0][0] <= number - 2 else []
        dq, *terms = group_gradients(
            first_tail, order, queries, output_gradient,
            saved_output, saved_key_rows, saved_value_rows, (peer_kv[at], kv_first), (own_tail, 0),
            (before_kv[at], kv_first), first, count, dq, terms, terms_first, terms_count, others,
        )
        if first + count == terms_first + terms_count:
            own_terms, peer_terms, tail_terms = terms
            back_terms = shifted(tail_terms, "ctx", -1)
            waiting.append((number, terms_first, own_terms, peer_terms, back_terms))
            terms = [None] * 3
    while waiting:
        if len(waiting) == 1:
            while len(sent) > LATE:
                outs = total(outs)
        send(*(outs or ()))
    while sent:
        outs = total(outs)
    return (dq, *outs)


def solution(mesh):
    tokens = P(("ctx", "head"), None)
    return jax.shard_map(
        body,
        mesh=mesh,
        in_specs=(tokens, tokens, tokens, tokens, tokens, P("ctx", None)),
        out_specs=(tokens, tokens, tokens),
        check_vma=False,
    )
```
